768 devices in a mesh: row: 6 (over z_hi, core), col: 128 (over z_lo, x, y).
Axes of the slice: x: 4, y: 8, z: 12 (z_hi: 3, z_lo: 4; z = z_hi * 4 + z_lo), core: 2. Of those that a mesh axis runs over, the one named last changes fastest.
Arguments:
- tokens: bfloat16 [816, 8192], P('row', 'col'), may hold values from -6 to 6
- w_in: bfloat16 [8192, 24576], P(None, 'col'), may hold values from -0.0625 to 0.0625
- short_filter: float32 [3, 24576], P(None, 'col'), may hold values from -3.5 to 3.5
- mr_filter: float32 [512, 128], P('col'), may hold values from -0.5 to 0.5
- skip: float32 [8192], P('col'), may hold values from 0.5 to 1.5
- w_out: bfloat16 [8192, 8192], P(None, 'col'), may hold values from -0.0625 to 0.0625
- grad_out: bfloat16 [816, 8192], P('row', 'col'), may hold values from -0.119628906 to 0.119628906
Outputs:
- block_out: bfloat16 [816, 8192], P('row', 'col')
- filter_grad: float32 [512, 128], P('col')
- skip_grad: float32 [8192], P('col')
The draws below stay inside these ranges and needn't reach their ends.
All inputs are finite; a program needn't handle non-finite values.
Results may differ from the reference program's by a relative error of at most 0.0085.
Values may be sent and summed in bfloat16 or wider, within the bound.
A program may use at most 64 MiB of HBM per device.

```python
import jax
import jax.numpy as jnp
from jax import lax

D = 8192
GSIZE = 16
TAPS = 128
GROUPS = 512
SEQ = 816


def level_of(stream_key, extent, cuts, least, top_value):
    def one(axis_at, blocks):
        heights = jax.random.uniform(jax.random.fold_in(jax.random.fold_in(stream_key, 6), axis_at), (blocks,), jnp.float32, least / len(cuts), top_value / len(cuts))
        return jnp.repeat(jnp.exp(heights), extent[axis_at] // blocks).reshape((-1,) + (1,) * (len(extent) - axis_at - 1))

    level = one(*cuts[0])
    for cut in cuts[1:]:
        level = level * one(*cut)
    return level


def normal_values(stream_key, extent, spread, limit, shards=(), held_as=jnp.bfloat16):
    entries = spread * jax.random.normal(stream_key, extent, jnp.float32)
    if shards:
        entries = entries * level_of(stream_key, extent, shards, -0.22, 0.18)
    return jnp.clip(entries, -limit, limit).astype(held_as)


def setup_inputs(seed: int = 0) -> dict:
    key_of = jax.random.split(jax.random.key(seed), 8)
    tokens = normal_values(key_of[0], (SEQ, D), 1.0, 6.0, ((0, 6), (1, 128)))
    w_in = normal_values(key_of[1], (D, 3 * D), D ** -0.5, 0.0625, ((1, 128),))
    short_filter = normal_values(key_of[2], (3, 3 * D), 3 ** -0.5, 3.5, ((1, 128),), jnp.float32)
    mr_filter = normal_values(key_of[3], (GROUPS, TAPS), TAPS ** -0.5, 0.5, ((0, 128),), jnp.float32)
    skip = jnp.clip(0.5 + 1.0 * jax.random.uniform(key_of[4], (D,), jnp.float32) ** level_of(key_of[4], (D,), ((0, 128),), -0.2, 0.2), 0.5, 1.5)
    w_out = normal_values(key_of[5], (D, D), D ** -0.5, 0.0625, ((1, 128),))
    grad_out = normal_values(key_of[6], (SEQ, D), 0.02, 0.119628906, ((0, 6), (1, 128)))
    return dict(tokens=tokens, w_in=w_in, short_filter=short_filter, mr_filter=mr_filter, skip=skip, w_out=w_out, grad_out=grad_out)


def reference(tokens, w_in, short_filter, mr_filter, skip, w_out, grad_out):
    seq_len = tokens.shape[0]
    projected = jnp.dot(tokens, w_in, preferred_element_type=jnp.float32).astype(jnp.bfloat16)
    projected = lax.optimization_barrier(projected).astype(jnp.float32)
    padded = jnp.pad(projected, ((2, 0), (0, 0)))
    short = short_filter[0] * padded[2:] + short_filter[1] * padded[1:-1] + short_filter[2] * padded[:-2]
    branches = short.reshape(seq_len, GROUPS, 3, GSIZE)
    query = branches[:, :, 0, :].reshape(seq_len, D)
    mixed = (branches[:, :, 1, :] * branches[:, :, 2, :]).reshape(seq_len, D)
    mixed_pad = jnp.pad(mixed, ((TAPS - 1, 0), (0, 0)))
    tap_table = jnp.repeat(mr_filter, GSIZE, axis=0).T

    def add_tap(step, running):
        window = lax.dynamic_slice_in_dim(mixed_pad, TAPS - 1 - step, seq_len, 0)
        return running + tap_table[step] * window
    longconv = lax.fori_loop(0, TAPS, add_tap, jnp.zeros((seq_len, D), jnp.float32))
    gated = (query * (longconv + skip * mixed)).astype(jnp.bfloat16)
    block_out = jnp.dot(gated, w_out, preferred_element_type=jnp.float32).astype(jnp.bfloat16)
    grad_gated = jnp.dot(grad_out, w_out.T, preferred_element_type=jnp.float32)
    weighted = grad_gated * query

    def tap_grad(step):
        window = lax.dynamic_slice_in_dim(mixed_pad, TAPS - 1 - step, seq_len, 0)
        return lax.optimization_barrier(jnp.sum((weighted * window).reshape(seq_len, GROUPS, GSIZE), axis=(0, 2)))
    filter_grad = lax.map(tap_grad, jnp.arange(TAPS, dtype=jnp.int32)).T
    skip_grad = lax.optimization_barrier(jnp.sum(weighted * mixed, axis=0))
    return (block_out, filter_grad, skip_grad)
```

```python
import jax
import jax.numpy as jnp
from jax import lax
from jax.experimental import pallas as pl
from jax.experimental.pallas import tpu as pltpu
from jax.sharding import PartitionSpec as P

MESH = pl.DeviceIdType.MESH
NX, NY, NZ, NR = 4, 8, 4, 6
NP = NX * NY
ROWS = 136
PAD = 144
CUT = 80
CUT2 = 64
TAPS = 128
WIDE = 384
BF = jnp.bfloat16
F32 = jnp.float32
HIGH = lax.Precision.HIGHEST
NSEM = 160


class Comm:
    def __init__(self, ss, rs):
        self.ss, self.rs, self.count, self.started = ss, rs, 0, []

    def send(self, src, dst, dev):
        i = self.count
        self.count += 1
        copy = pltpu.make_async_remote_copy(
            src_ref=src,
            dst_ref=dst,
            send_sem=self.ss.at[i],
            recv_sem=self.rs.at[i],
            device_id=dev,
            device_id_type=MESH,
        )
        copy.start()
        self.started.append(copy)
        return (i, dev)

    def arrive(self, handle, dst):
        i, dev = handle
        pltpu.make_async_remote_copy(
            src_ref=dst,
            dst_ref=dst,
            send_sem=self.ss.at[i],
            recv_sem=self.rs.at[i],
            device_id=dev,
            device_id_type=MESH,
        ).wait_recv()

    def finish(self):
        for copy in self.started:
            copy.wait_send()


def iota(shape, dim):
    return lax.broadcasted_iota(jnp.int32, shape, dim)


def swap(v):
    return pltpu.roll(v, 64, 1)


def low(v):
    return iota(v.shape, 1) < 64


def lows(a, b):
    return jnp.where(low(a), a, swap(b))


def highs(a, b):
    return jnp.where(low(a), swap(a), b)


def pack(tile, half):
    top = tile[:CUT]
    rest = jnp.concatenate([tile[CUT:], jnp.zeros((2 * CUT - PAD, 128), F32)], 0)
    return lows(top, rest) if half == 0 else highs(top, rest)


def unpack(v):
    up = swap(v)
    full = jnp.concatenate([v, up[: PAD - CUT]], 0)
    return jnp.where(low(full), full, 0.0)


def dot(a, b):
    return jnp.dot(a, b, preferred_element_type=F32)


def dot_t(a, b):
    return lax.dot_general(a, b, (((1,), (1,)), ((), ())), preferred_element_type=F32)


def kernel(
    tok, grd, win, sfl, flt, skp, wout,
    out_ref, fg_ref, sg_ref,
    wv, wov, zr, gath, wpk, wrv, wz, acc, gz, gp, gr, yp, yr, hs, hr, pb, h2r, gated, op, orv, pr, toep,
    ss, rs, ls,
):
    r = lax.axis_index("row")
    c = lax.axis_index("col")
    core = r % 2
    z = c // NP
    x = (c // NY) % NX
    y = c % NY
    sgn = 1 - 2 * core
    comm = Comm(ss, rs)

    def at(dx=0, dy=0, dz=0):
        return (r, ((z + dz + NZ) % NZ) * NP + ((x + dx + NX) % NX) * NY + (y + dy + NY) % NY)

    def chunk(dx, dy):
        return ((x - dx + NX) % NX) * NY + (y - dy + NY) % NY

    def by_row(i):
        return ((r + i) % NR, c)

    sibling = (r + sgn, c)
    own = chunk(0, 0)

    loads = [pltpu.make_async_copy(wout, wov, ls.at[0])]
    for k in range(NZ):
        loads.append(pltpu.make_async_copy(win.at[k], wv.at[:, pl.ds(64 * k, 64), :], ls.at[1 + k]))
    for load in loads:
        load.start()

    peers = [at(dz=i) for i in range(1, NZ)] + [at(dx=i) for i in range(1, NX)]
    peers += [at(dy=i) for i in range(1, NY)] + [by_row(i) for i in range(1, NR)]
    barrier = pltpu.get_barrier_semaphore()
    for peer in peers:
        pl.semaphore_signal(barrier, inc=1, device_id=peer, device_id_type=MESH)

    both = jnp.concatenate([tok[...].astype(F32), grd[...].astype(F32)], 1)
    zr[z] = jnp.concatenate([both, jnp.zeros((PAD - ROWS, 128), F32)], 0).astype(BF)

    pl.semaphore_wait(barrier, len(peers))

    z_moves = [comm.send(zr.at[z], zr.at[z], at(dz=i)) for i in (1, 2, 3)]

    loads[0].wait()
    half = pl.multiple_of(core * 512, 512)
    w_moves = []
    for i in (1, 2, 3):
        base = pl.multiple_of(((z + i) % NZ) * 2048 + core * 512, 512)
        a = wov[pl.ds(base, 512), :].astype(F32)
        b = wov[pl.ds(base + 1024, 512), :].astype(F32)
        wpk[i - 1] = jnp.concatenate([a, b], 1).astype(BF)
        w_moves.append(comm.send(wpk.at[i - 1], wrv.at[z, pl.ds(half, 512)], at(dz=i)))
    mine = pl.multiple_of(z * 2048, 2048)
    wrv[z] = jnp.concatenate(
        [wov[pl.ds(mine, 1024), :].astype(F32), wov[pl.ds(mine + 1024, 1024), :].astype(F32)], 1
    ).astype(BF)

    col = iota((192, WIDE), 1)
    lane = col & 127
    source = (lane >> 4) * 48 + (col >> 7) * 16 + (lane & 15)
    hit = (iota((192, WIDE), 0) == source) & (lane < 64)
    perm = jnp.where(hit, 1.0, 0.0)
    short_taps = jnp.dot(sfl[...], perm, precision=HIGH, preferred_element_type=F32)
    perm_b = perm.astype(BF)

    place = jnp.where((iota((TAPS, WIDE), 0) + iota((TAPS, WIDE), 1)) % WIDE == 0, 1.0, 0.0).astype(BF)
    taps0 = dot(flt[...].astype(BF), place)
    for g in range(4):
        line = jnp.broadcast_to(taps0[g : g + 1], (PAD, WIDE))
        toep[pl.ds(g * PAD, PAD)] = pltpu.roll(line, 0, 1, stride=1, stride_axis=0).astype(BF)

    for load in loads[1:]:
        load.wait()
    for i, move in zip((1, 2, 3), z_moves):
        comm.arrive(move, zr.at[(z - i + NZ) % NZ])
    q0, q1, q2, q3 = [zr[k].astype(F32) for k in range(NZ)]
    gath[own] = jnp.concatenate([lows(q0, q1), lows(q2, q3)], 1).astype(BF)
    gz[...] = jnp.concatenate([highs(q0, q1), highs(q2, q3)], 1).astype(BF)

    parts = {"A": pl.ds(0, CUT), "B": pl.ds(CUT, PAD - CUT)}
    moves = {}

    def pass_on(part, dx, dy, to_dx, to_dy, step_x, step_y):
        ref = gath.at[chunk(dx, dy), parts[part]]
        moves[part, to_dx, to_dy] = comm.send(ref, ref, at(dx=step_x, dy=step_y))

    def y_steps(part, dx, dy):
        if 0 <= dy <= 2:
            pass_on(part, dx, dy, dx, dy + 1, 0, 1)
        if -2 <= dy <= 0:
            pass_on(part, dx, dy, dx, dy - 1, 0, -1)
        if dy == -3:
            pass_on(part, dx, 3 * sgn, dx, 4, 0, sgn)

    def x_steps(part, dx, dy):
        if dx == 0:
            pass_on(part, 0, dy, 1, dy, 1, 0)
            pass_on(part, 0, dy, -1, dy, -1, 0)
        if dx == -1:
            pass_on(part, sgn, dy, 2, dy, sgn, 0)

    def forward(part, dx, dy):
        if part == "A":
            if dx == 0:
                y_steps(part, 0, dy)
            x_steps(part, dx, dy)
        else:
            if dy == 0:
                x_steps(part, dx, 0)
            y_steps(part, dx, dy)

    order = sorted(
        [(dx, dy) for dx in (0, 1, -1, 2) for dy in (0, 1, -1, 2, -2, 3, -3, 4)],
        key=lambda d: (abs(d[0]) + abs(d[1]), abs(d[0]), -d[0], -d[1]),
    )
    forward("A", 0, 0)
    forward("B", 0, 0)

    def project(places):
        total = None
        for dx, dy in places:
            p = chunk(dx, dy)
            term = dot(gath[p], wv[p])
            total = term if total is None else total + term
        return total

    acc[...] = project([(0, 0)])
    w_back = []
    for hop in range(1, 7):
        places = [d for d in order if abs(d[0]) + abs(d[1]) == hop]
        for dx, dy in places:
            for part in ("A", "B"):
                comm.arrive(moves[part, dx, dy], gath.at[chunk(dx, dy), parts[part]])
                forward(part, dx, dy)
        if hop == 4:
            for i, move in zip((1, 2, 3), w_moves):
                ref = wrv.at[(z - i + NZ) % NZ, pl.ds(half, 512)]
                comm.arrive(move, ref)
                w_back.append(comm.send(ref, ref, sibling))
        acc[...] += project(places)

    proj = dot(acc[...].astype(BF), perm_b)
    pb[...] = proj.astype(BF)
    tail_move = comm.send(pb.at[pl.ds(128, 16)], h2r, by_row(1))
    t = iota((PAD, WIDE), 0)
    one = jnp.where(t >= 1, pltpu.roll(proj, 1, 0), 0.0)
    two = jnp.where(t >= 2, pltpu.roll(proj, 2, 0), 0.0)
    s0, s1, s2 = short_taps[0:1], short_taps[1:2], short_taps[2:3]
    short = s0 * proj + s1 * one + s2 * two
    live = iota((PAD, 128), 0) < ROWS
    mixed = jnp.where(live, short[:, 128:256] * short[:, 256:384], 0.0)
    hs[...] = lows(mixed[8:72], mixed[72:136]).astype(BF)
    halo_move = comm.send(hs, hr, by_row(1))

    other = pl.multiple_of(512 - core * 512, 512)
    for i, move in zip((1, 2, 3), w_back):
        comm.arrive(move, wrv.at[(z - i + NZ) % NZ, pl.ds(other, 512)])

    def build(i, carry):
        at_row = pl.multiple_of(i * 128, 128)
        w0, w1, w2, w3 = [wrv[k, pl.ds(at_row, 128), :].astype(F32) for k in range(NZ)]
        wz[pl.ds(at_row, 128), :] = jnp.concatenate([lows(w0, w1), lows(w2, w3)], 1).astype(BF)
        wz[pl.ds(at_row + 1024, 128), :] = jnp.concatenate([highs(w0, w1), highs(w2, w3)], 1).astype(BF)
        return carry

    lax.fori_loop(0, 8, build, 0)
    for k in range(NX):
        gp[k] = dot_t(gz[...], wz[pl.ds(512 * k, 512), :]).astype(BF)
    gx_moves = [comm.send(gp.at[(x + i) % NX], gr.at[x], at(dx=i)) for i in (1, 3, 2)]

    comm.arrive(tail_move, h2r)
    last = jnp.where(r > 0, h2r[...].astype(F32), 0.0)
    before1, before2 = last[7:8], last[6:7]
    t8 = iota((8, WIDE), 0)
    fix = jnp.where(t8 == 0, s1 * before1 + s2 * before2, jnp.where(t8 == 1, s2 * before1, 0.0))
    short = jnp.concatenate([short[:8] + fix, short[8:]], 0)
    query = short[:, :128]
    mixed = jnp.where(live, short[:, 128:256] * short[:, 256:384], 0.0)
    own_b = jnp.concatenate([mixed, jnp.zeros((256 - PAD, 128), F32)], 0).astype(BF)
    near = dot(toep[:, :256], own_b)
    comm.arrive(halo_move, hr)
    h = jnp.where(r > 0, hr[...].astype(F32), 0.0)
    prev = jnp.concatenate([jnp.where(low(h), h, 0.0), jnp.where(low(h), swap(h), 0.0)], 0)
    prev_b = prev.astype(BF)
    big = near + dot(toep[:, 256:], prev_b)
    group = iota((PAD, 128), 1) >> 4
    conv = jnp.zeros((PAD, 128), F32)
    for g in range(4):
        conv = jnp.where(group == g, big[g * PAD : (g + 1) * PAD], conv)
    skip = jnp.concatenate([skp[...], jnp.zeros((1, 64), F32)], 1)
    value = query * (conv + skip * mixed)
    gated[own] = pack(value, 0).astype(BF)

    parts2 = {"A": pl.ds(0, CUT2), "B": pl.ds(CUT2, CUT - CUT2)}
    moves2 = {}
    ys, xs = (1, 7, 2, 6, 3, 5, 4), (1, 3, 2)

    def direct(part, dx, dy, step_x, step_y):
        ref = gated.at[chunk(dx, dy), parts2[part]]
        moves2[part, dx + step_x, dy + step_y] = comm.send(ref, ref, at(dx=step_x, dy=step_y))

    for dy in ys:
        direct("A", 0, 0, 0, dy)
    for dx in xs:
        direct("B", 0, 0, dx, 0)
        direct("A", 0, 0, dx, 0)
    for dy in ys:
        direct("B", 0, 0, 0, dy)

    total = gp[x].astype(F32)
    for i, move in zip((1, 3, 2), gx_moves):
        comm.arrive(move, gr.at[(x - i + NX) % NX])
        total = total + gr[(x - i + NX) % NX].astype(F32)
    for k in range(NY):
        yp[k] = pack(total[:, 128 * (k // 2) : 128 * (k // 2) + 128], k % 2).astype(BF)

    for dx in xs:
        comm.arrive(moves2["B", dx, 0], gated.at[chunk(dx, 0), parts2["B"]])
        for dy in ys:
            direct("B", dx, 0, 0, dy)
    for dy in ys:
        comm.arrive(moves2["A", 0, dy], gated.at[chunk(0, dy), parts2["A"]])
        for dx in xs:
            direct("A", 0, dy, dx, 0)
    gy_moves = [comm.send(yp.at[(y + i) % NY], yr.at[y], at(dy=i)) for i in ys]

    grad = unpack(yp[y].astype(F32))
    for i, move in zip(ys, gy_moves):
        comm.arrive(move, yr.at[(y - i + NY) % NY])
        grad = grad + unpack(yr[(y - i + NY) % NY].astype(F32))
    weighted = jnp.where(live, grad * query, 0.0)
    skip_part = jnp.sum(weighted * mixed, axis=0, keepdims=True)
    flip = jnp.where(iota((PAD, PAD), 0) + iota((PAD, PAD), 1) == PAD - 1, 1.0, 0.0).astype(BF)
    back = dot(flip, weighted.astype(BF))
    stack = jnp.concatenate([jnp.where(group == g, back, 0.0) for g in range(4)], 0).astype(BF)
    ext = jnp.concatenate([own_b, prev_b], 0)
    corr = dot_t(stack, ext)
    lines = [
        jnp.sum(
            pltpu.roll(corr[g * PAD : (g + 1) * PAD], 0, 1, stride=1, stride_axis=0), axis=0, keepdims=True
        )
        for g in range(4)
    ]
    lines = jnp.concatenate(lines + [jnp.zeros((4, WIDE), F32)], 0)
    pick = jnp.where(iota((WIDE, TAPS), 0) + iota((WIDE, TAPS), 1) == PAD - 1, 1.0, 0.0)
    tap_part = jnp.dot(lines, pick, precision=HIGH, preferred_element_type=F32)
    pr[r] = jnp.where(iota((8, 128), 0) == 4, skip_part, tap_part)
    row_moves = [comm.send(pr.at[r], pr.at[r], by_row(i)) for i in range(1, NR)]

    for dx in xs:
        comm.arrive(moves2["A", dx, 0], gated.at[chunk(dx, 0), parts2["A"]])
    for dy in ys:
        comm.arrive(moves2["B", 0, dy], gated.at[chunk(0, dy), parts2["B"]])
    for dy in ys:
        for dx in xs:
            for part in ("A", "B"):
                comm.arrive(moves2[part, dx, dy], gated.at[chunk(dx, dy), parts2[part]])
    outp = jnp.zeros((PAD, 256), F32)
    for k in range(NP // 4):
        u0, u1, u2, u3 = [gated[4 * k + i].astype(F32) for i in range(4)]
        top = jnp.concatenate([lows(u0, u1), lows(u2, u3)], 1)
        rest = jnp.concatenate([highs(u0, u1), highs(u2, u3)], 1)[: PAD - CUT]
        outp = outp + dot(jnp.concatenate([top, rest], 0).astype(BF), wz[pl.ds(256 * k, 256), :])
    for k in range(NZ):
        op[k] = pack(outp[:, 128 * (k // 2) : 128 * (k // 2) + 128], k % 2).astype(BF)
    o_moves = [comm.send(op.at[(z + i) % NZ], orv.at[z], at(dz=i)) for i in (1, 2, 3)]
    result = op[z].astype(F32)
    for i, move in zip((1, 2, 3), o_moves):
        comm.arrive(move, orv.at[(z - i + NZ) % NZ])
        result = result + orv[(z - i + NZ) % NZ].astype(F32)
    out_ref[...] = unpack(result)[:ROWS, :64].astype(BF)

    for i, move in zip(range(1, NR), row_moves):
        comm.arrive(move, pr.at[(r - i + NR) % NR])
    sums = pr[0]
    for k in range(1, NR):
        sums = sums + pr[k]
    fg_ref[...] = sums[:4]
    sg_ref[...] = sums[4:5, :64]
    comm.finish()
    assert comm.count <= NSEM


def local(tokens, w_in, short_filter, mr_filter, skip, w_out, grad_out):
    vmem = pl.BlockSpec(memory_space=pltpu.VMEM)
    hbm = pl.BlockSpec(memory_space=pl.ANY)
    scratch = [
        pltpu.VMEM((NP, 256, 192), BF),
        pltpu.VMEM((8192, 64), BF),
        pltpu.VMEM((NZ, PAD, 128), BF),
        pltpu.VMEM((NP, PAD, 256), BF),
        pltpu.VMEM((NZ - 1, 512, 128), BF),
        pltpu.VMEM((NZ, 1024, 128), BF),
        pltpu.VMEM((2048, 256), BF),
        pltpu.VMEM((PAD, 192), F32),
        pltpu.VMEM((PAD, 256), BF),
        pltpu.VMEM((NX, PAD, 512), BF),
        pltpu.VMEM((NX, PAD, 512), BF),
        pltpu.VMEM((NY, CUT, 128), BF),
        pltpu.VMEM((NY, CUT, 128), BF),
        pltpu.VMEM((64, 128), BF),
        pltpu.VMEM((64, 128), BF),
        pltpu.VMEM((PAD, WIDE), BF),
        pltpu.VMEM((16, WIDE), BF),
        pltpu.VMEM((NP, CUT, 128), BF),
        pltpu.VMEM((NZ, CUT, 128), BF),
        pltpu.VMEM((NZ, CUT, 128), BF),
        pltpu.VMEM((NR, 8, 128), F32),
        pltpu.VMEM((4 * PAD, WIDE), BF),
        pltpu.SemaphoreType.DMA((NSEM,)),
        pltpu.SemaphoreType.DMA((NSEM,)),
        pltpu.SemaphoreType.DMA((1 + NZ,)),
    ]
    out, taps, gains = pl.pallas_call(
        kernel,
        out_shape=(
            jax.ShapeDtypeStruct((ROWS, 64), BF),
            jax.ShapeDtypeStruct((4, TAPS), F32),
            jax.ShapeDtypeStruct((1, 64), F32),
        ),
        in_specs=[vmem, vmem, hbm, vmem, vmem, vmem, hbm],
        out_specs=(vmem, vmem, vmem),
        scratch_shapes=scratch,
        compiler_params=pltpu.CompilerParams(
            collective_id=0, has_side_effects=True, vmem_limit_bytes=56 * 1024 * 1024
        ),
        name="hyena_block",
    )(tokens, grad_out, w_in.reshape(NZ, NP, 64, 192), short_filter, mr_filter, skip.reshape(1, 64), w_out)
    return out, taps, gains.reshape(64)


def solution(mesh):
    in_specs = (
        P("row", "col"),
        P(None, "col"),
        P(None, "col"),
        P("col", None),
        P("col"),
        P(None, "col"),
        P("row", "col"),
    )
    out_specs = (P("row", "col"), P("col", None), P("col"))
    return jax.shard_map(local, mesh=mesh, in_specs=in_specs, out_specs=out_specs, check_vma=False)
```

```python
import jax
import jax.numpy as jnp
from jax import lax
from jax.experimental import pallas as pl
from jax.experimental.pallas import tpu as pltpu
from jax.sharding import PartitionSpec as P

MESH = pl.DeviceIdType.MESH
NX, NY, NZ, NR = 4, 8, 4, 6
NP = NX * NY
ROWS = 136
PAD = 144
CUT = 80
CUT2 = 64
TAPS = 128
WIDE = 384
BF = jnp.bfloat16
F32 = jnp.float32
HIGH = lax.Precision.HIGHEST
NSEM = 160


class Comm:
    def __init__(self, ss, rs):
        self.ss, self.rs, self.count, self.started = ss, rs, 0, []

    def send(self, src, dst, dev):
        i = self.count
        self.count += 1
        copy = pltpu.make_async_remote_copy(
            src_ref=src,
            dst_ref=dst,
            send_sem=self.ss.at[i],
            recv_sem=self.rs.at[i],
            device_id=dev,
            device_id_type=MESH,
        )
        copy.start()
        self.started.append(copy)
        return (i, dev)

    def arrive(self, handle, dst):
        i, dev = handle
        pltpu.make_async_remote_copy(
            src_ref=dst,
            dst_ref=dst,
            send_sem=self.ss.at[i],
            recv_sem=self.rs.at[i],
            device_id=dev,
            device_id_type=MESH,
        ).wait_recv()

    def finish(self):
        for copy in self.started:
            copy.wait_send()


def iota(shape, dim):
    return lax.broadcasted_iota(jnp.int32, shape, dim)


def swap(v):
    return pltpu.roll(v, 64, 1)


def low(v):
    return iota(v.shape, 1) < 64


def lows(a, b):
    return jnp.where(low(a), a, swap(b))


def highs(a, b):
    return jnp.where(low(a), swap(a), b)


def pack(tile, half):
    top = tile[:CUT]
    rest = jnp.concatenate([tile[CUT:], jnp.zeros((2 * CUT - PAD, 128), F32)], 0)
    return lows(top, rest) if half == 0 else highs(top, rest)


def unpack(v):
    up = swap(v)
    full = jnp.concatenate([v, up[: PAD - CUT]], 0)
    return jnp.where(low(full), full, 0.0)


def dot(a, b):
    return jnp.dot(a, b, preferred_element_type=F32)


def dot_t(a, b):
    return lax.dot_general(a, b, (((1,), (1,)), ((), ())), preferred_element_type=F32)


def kernel(
    tok_in, grd_in, win, sfl_in, flt_in, skp_in, wout,
    res_ref,
    tok, grd, sfl, flt, skp, wraw, wv, zr, gath, wz, acc, gz, gp, gr, yp, yr, hs, hr, pb, h2r, gated, op, orv, pr, toep,
    ss, rs, ls,
):
    r = lax.axis_index("row")
    c = lax.axis_index("col")
    core = r % 2
    z = c // NP
    x = (c // NY) % NX
    y = c % NY
    sgn = 1 - 2 * core
    comm = Comm(ss, rs)

    def at(dx=0, dy=0, dz=0):
        return (r, ((z + dz + NZ) % NZ) * NP + ((x + dx + NX) % NX) * NY + (y + dy + NY) % NY)

    def chunk(dx, dy):
        return ((x - dx + NX) % NX) * NY + (y - dy + NY) % NY

    def by_row(i):
        return ((r + i) % NR, c)

    sibling = (r + sgn, c)
    own = chunk(0, 0)

    peers = [at(dz=i) for i in range(1, NZ)] + [at(dx=i) for i in range(1, NX)]
    peers += [at(dy=i) for i in range(1, NY)] + [by_row(i) for i in range(1, NR)]
    barrier = pltpu.get_barrier_semaphore()
    for peer in peers:
        pl.semaphore_signal(barrier, inc=1, device_id=peer, device_id_type=MESH)

    mine = pl.multiple_of(z * 2048, 2048)
    keep = pl.multiple_of(z * 64, 64)
    pairs = [(tok_in, tok), (grd_in, grd), (sfl_in, sfl), (flt_in, flt), (skp_in, skp), (win, wraw)]
    pairs.append((wout.at[:, pl.ds(mine, 2048)], wz.at[pl.ds(keep, 64)]))
    loads = [pltpu.make_async_copy(a, b, ls.at[i]) for i, (a, b) in enumerate(pairs)]
    for load in loads:
        load.start()
    loads[0].wait()
    loads[1].wait()
    both = jnp.concatenate([tok[...].astype(F32), grd[...].astype(F32)], 0)
    both = jnp.concatenate([both, jnp.zeros((128, 256 - ROWS), F32)], 1)
    zr[z] = both.T[:PAD].astype(BF)

    pl.semaphore_wait(barrier, len(peers))

    z_moves = [comm.send(zr.at[z], zr.at[z], at(dz=i)) for i in (1, 2, 3)]

    col = iota((192, WIDE), 1)
    lane = col & 127
    source = (lane >> 4) * 48 + (col >> 7) * 16 + (lane & 15)
    hit = (iota((192, WIDE), 0) == source) & (lane < 64)
    perm = jnp.where(hit, 1.0, 0.0)
    loads[2].wait()
    loads[3].wait()
    short_taps = jnp.dot(sfl[...], perm, precision=HIGH, preferred_element_type=F32)
    perm_b = perm.astype(BF)

    place = jnp.where((iota((TAPS, WIDE), 0) + iota((TAPS, WIDE), 1)) % WIDE == 0, 1.0, 0.0).astype(BF)
    taps0 = dot(flt[...].astype(BF), place)
    for g in range(4):
        line = jnp.broadcast_to(taps0[g : g + 1], (PAD, WIDE))
        toep[pl.ds(g * PAD, PAD)] = pltpu.roll(line, 0, 1, stride=1, stride_axis=0).astype(BF)

    loads[5].wait()

    def reorder(pair, carry):
        tiles = [wraw[:, pl.ds(pl.multiple_of(k * 2048 + pair * 128, 128), 128)] for k in range(NZ)]
        t0, t1, t2, t3 = [v.astype(F32) for v in tiles]
        wv[2 * pair] = jnp.concatenate([lows(t0, t1), lows(t2, t3)], 1).astype(BF)
        wv[2 * pair + 1] = jnp.concatenate([highs(t0, t1), highs(t2, t3)], 1).astype(BF)
        return carry

    lax.fori_loop(0, NP // 2, reorder, 0)
    for i, move in zip((1, 2, 3), z_moves):
        comm.arrive(move, zr.at[(z - i + NZ) % NZ])
    half = pl.multiple_of(core * 1024, 1024)
    w_moves = []
    for i in (1, 2, 3):
        base = pl.multiple_of(((z + i) % NZ) * 2048 + core * 1024, 1024)
        w_moves.append(
            comm.send(wout.at[:, pl.ds(base, 1024)], wz.at[pl.ds(keep, 64), pl.ds(half, 1024)], at(dz=i))
        )

    q0, q1, q2, q3 = [zr[k].astype(F32) for k in range(NZ)]
    gath[own] = jnp.concatenate([lows(q0, q1), lows(q2, q3)], 1).astype(BF)
    gz[...] = jnp.concatenate([highs(q0, q1), highs(q2, q3)], 1).astype(BF)

    parts = {"A": pl.ds(0, CUT), "B": pl.ds(CUT, PAD - CUT)}
    moves = {}

    def pass_on(part, dx, dy, to_dx, to_dy, step_x, step_y):
        ref = gath.at[chunk(dx, dy), parts[part]]
        moves[part, to_dx, to_dy] = comm.send(ref, ref, at(dx=step_x, dy=step_y))

    def y_steps(part, dx, dy):
        if 0 <= dy <= 2:
            pass_on(part, dx, dy, dx, dy + 1, 0, 1)
        if -2 <= dy <= 0:
            pass_on(part, dx, dy, dx, dy - 1, 0, -1)
        if dy == -3:
            pass_on(part, dx, 3 * sgn, dx, 4, 0, sgn)

    def x_steps(part, dx, dy):
        if dx == 0:
            pass_on(part, 0, dy, 1, dy, 1, 0)
            pass_on(part, 0, dy, -1, dy, -1, 0)
            pass_on(part, 0, dy, 2, dy, 2, 0)

    def forward(part, dx, dy):
        if part == "A":
            if dx == 0:
                y_steps(part, 0, dy)
            x_steps(part, dx, dy)
        else:
            if dy == 0:
                x_steps(part, dx, 0)
            y_steps(part, dx, dy)

    def hops(d):
        return min(abs(d[0]), 1) + abs(d[1])

    order = sorted(
        [(dx, dy) for dx in (0, 1, -1, 2) for dy in (0, 1, -1, 2, -2, 3, -3, 4)],
        key=lambda d: (hops(d), abs(d[0]), -d[0], -d[1]),
    )
    forward("A", 0, 0)
    forward("B", 0, 0)

    def project(places):
        total = None
        for dx, dy in places:
            p = chunk(dx, dy)
            term = dot_t(gath[p], wv[p])
            total = term if total is None else total + term
        return total

    acc[...] = project([(0, 0)])
    w_back = []
    gx_moves = []

    def sum_over_x():
        loads[6].wait()
        other = pl.multiple_of(1024 - core * 1024, 1024)
        for i, move in zip((1, 2, 3), w_back):
            comm.arrive(move, wz.at[pl.ds(pl.multiple_of(((z - i + NZ) % NZ) * 64, 64), 64), pl.ds(other, 1024)])
        for k in range(NX):
            gp[k] = dot(gz[...], wz[:, pl.ds(512 * k, 512)]).astype(BF)
        for i in (1, 3, 2):
            gx_moves.append(comm.send(gp.at[(x + i) % NX], gr.at[x], at(dx=i)))

    for hop in range(1, 6):
        places = [d for d in order if hops(d) == hop]
        for dx, dy in places:
            for part in ("A", "B"):
                comm.arrive(moves[part, dx, dy], gath.at[chunk(dx, dy), parts[part]])
                forward(part, dx, dy)
        if hop == 3:
            for i, move in zip((1, 2, 3), w_moves):
                ref = wz.at[pl.ds(pl.multiple_of(((z - i + NZ) % NZ) * 64, 64), 64), pl.ds(half, 1024)]
                comm.arrive(move, ref)
                w_back.append(comm.send(ref, ref, sibling))
        if hop == 4:
            sum_over_x()
        acc[...] += project(places)

    proj = dot(acc[...].astype(BF), perm_b)
    pb[...] = proj.astype(BF)
    tail_move = comm.send(pb.at[pl.ds(128, 16)], h2r, by_row(1))
    t = iota((PAD, WIDE), 0)
    one = jnp.where(t >= 1, pltpu.roll(proj, 1, 0), 0.0)
    two = jnp.where(t >= 2, pltpu.roll(proj, 2, 0), 0.0)
    s0, s1, s2 = short_taps[0:1], short_taps[1:2], short_taps[2:3]
    short = s0 * proj + s1 * one + s2 * two
    live = iota((PAD, 128), 0) < ROWS
    mixed = jnp.where(live, short[:, 128:256] * short[:, 256:384], 0.0)
    hs[...] = lows(mixed[8:72], mixed[72:136]).astype(BF)
    halo_move = comm.send(hs, hr, by_row(1))

    comm.arrive(tail_move, h2r)
    last = jnp.where(r > 0, h2r[...].astype(F32), 0.0)
    before1, before2 = last[7:8], last[6:7]
    t8 = iota((8, WIDE), 0)
    fix = jnp.where(t8 == 0, s1 * before1 + s2 * before2, jnp.where(t8 == 1, s2 * before1, 0.0))
    short = jnp.concatenate([short[:8] + fix, short[8:]], 0)
    query = short[:, :128]
    mixed = jnp.where(live, short[:, 128:256] * short[:, 256:384], 0.0)
    own_b = jnp.concatenate([mixed, jnp.zeros((256 - PAD, 128), F32)], 0).astype(BF)
    near = dot(toep[:, :256], own_b)
    comm.arrive(halo_move, hr)
    h = jnp.where(r > 0, hr[...].astype(F32), 0.0)
    prev = jnp.concatenate([jnp.where(low(h), h, 0.0), jnp.where(low(h), swap(h), 0.0)], 0)
    prev_b = prev.astype(BF)
    big = near + dot(toep[:, 256:], prev_b)
    group = iota((PAD, 128), 1) >> 4
    conv = jnp.zeros((PAD, 128), F32)
    for g in range(4):
        conv = jnp.where(group == g, big[g * PAD : (g + 1) * PAD], conv)
    loads[4].wait()
    skip = jnp.concatenate([skp[...], jnp.zeros((1, 64), F32)], 1)
    value = query * (conv + skip * mixed)
    gated[own] = pack(value, 0).astype(BF)

    parts2 = {"A": pl.ds(0, CUT2), "B": pl.ds(CUT2, CUT - CUT2)}
    moves2 = {}
    ys, xs = (1, 7, 2, 6, 3, 5, 4), (1, 3, 2)

    def direct(part, dx, dy, step_x, step_y):
        ref = gated.at[chunk(dx, dy), parts2[part]]
        moves2[part, dx + step_x, dy + step_y] = comm.send(ref, ref, at(dx=step_x, dy=step_y))

    for dy in ys:
        direct("A", 0, 0, 0, dy)
    for dx in xs:
        direct("B", 0, 0, dx, 0)
        direct("A", 0, 0, dx, 0)
    for dy in ys:
        direct("B", 0, 0, 0, dy)

    total = gp[x].astype(F32)
    for i, move in zip((1, 3, 2), gx_moves):
        comm.arrive(move, gr.at[(x - i + NX) % NX])
        total = total + gr[(x - i + NX) % NX].astype(F32)
    for k in range(NY):
        yp[k] = pack(total[:, 128 * (k // 2) : 128 * (k // 2) + 128], k % 2).astype(BF)

    for dx in xs:
        comm.arrive(moves2["B", dx, 0], gated.at[chunk(dx, 0), parts2["B"]])
        for dy in ys:
            direct("B", dx, 0, 0, dy)
    for dy in ys:
        comm.arrive(moves2["A", 0, dy], gated.at[chunk(0, dy), parts2["A"]])
        for dx in xs:
            direct("A", 0, dy, dx, 0)
    gy_moves = [comm.send(yp.at[(y + i) % NY], yr.at[y], at(dy=i)) for i in ys]

    grad = unpack(yp[y].astype(F32))
    for i, move in zip(ys, gy_moves):
        comm.arrive(move, yr.at[(y - i + NY) % NY])
        grad = grad + unpack(yr[(y - i + NY) % NY].astype(F32))
    weighted = jnp.where(live, grad * query, 0.0)
    skip_part = jnp.sum(weighted * mixed, axis=0, keepdims=True)
    flip = jnp.where(iota((PAD, PAD), 0) + iota((PAD, PAD), 1) == PAD - 1, 1.0, 0.0).astype(BF)
    back = dot(flip, weighted.astype(BF))
    stack = jnp.concatenate([jnp.where(group == g, back, 0.0) for g in range(4)], 0).astype(BF)
    ext = jnp.concatenate([own_b, prev_b], 0)
    corr = dot_t(stack, ext)
    lines = [
        jnp.sum(
            pltpu.roll(corr[g * PAD : (g + 1) * PAD], 0, 1, stride=1, stride_axis=0), axis=0, keepdims=True
        )
        for g in range(4)
    ]
    lines = jnp.concatenate(lines + [jnp.zeros((4, WIDE), F32)], 0)
    pick = jnp.where(iota((WIDE, TAPS), 0) + iota((WIDE, TAPS), 1) == PAD - 1, 1.0, 0.0)
    tap_part = jnp.dot(lines, pick, precision=HIGH, preferred_element_type=F32)
    pr[r] = jnp.where(iota((8, 128), 0) == 4, skip_part, tap_part)
    row_moves = [comm.send(pr.at[r], pr.at[r], by_row(i)) for i in range(1, NR)]

    for dx in xs:
        comm.arrive(moves2["A", dx, 0], gated.at[chunk(dx, 0), parts2["A"]])
    for dy in ys:
        comm.arrive(moves2["B", 0, dy], gated.at[chunk(0, dy), parts2["B"]])
    for dy in ys:
        for dx in xs:
            for part in ("A", "B"):
                comm.arrive(moves2[part, dx, dy], gated.at[chunk(dx, dy), parts2[part]])
    outp = jnp.zeros((PAD, 256), F32)
    for k in range(NP // 4):
        u0, u1, u2, u3 = [gated[4 * k + i].astype(F32) for i in range(4)]
        top = jnp.concatenate([lows(u0, u1), lows(u2, u3)], 1)
        rest = jnp.concatenate([highs(u0, u1), highs(u2, u3)], 1)[: PAD - CUT]
        outp = outp + dot_t(jnp.concatenate([top, rest], 0).astype(BF), wz[:, pl.ds(256 * k, 256)])
    for k in range(NZ):
        op[k] = pack(outp[:, 128 * (k // 2) : 128 * (k // 2) + 128], k % 2).astype(BF)
    o_moves = [comm.send(op.at[(z + i) % NZ], orv.at[z], at(dz=i)) for i in (1, 2, 3)]
    result = op[z].astype(F32)
    for i, move in zip((1, 2, 3), o_moves):
        comm.arrive(move, orv.at[(z - i + NZ) % NZ])
        result = result + orv[(z - i + NZ) % NZ].astype(F32)
    res_ref[pl.ds(0, ROWS)] = unpack(result)[:ROWS]

    for i, move in zip(range(1, NR), row_moves):
        comm.arrive(move, pr.at[(r - i + NR) % NR])
    sums = pr[0]
    for k in range(1, NR):
        sums = sums + pr[k]
    res_ref[pl.ds(ROWS, 8)] = sums
    comm.finish()
    assert comm.count <= NSEM


def split_results(res_ref, out_ref, fg_ref, sg_ref):
    block = jnp.concatenate([res_ref[pl.ds(0, ROWS)], jnp.zeros((256 - ROWS, 128), F32)], 0)
    out_ref[...] = block.T[:64, :ROWS].astype(BF)
    fg_ref[...] = res_ref[pl.ds(ROWS, 4)]
    sg_ref[...] = res_ref[pl.ds(ROWS + 4, 1), pl.ds(0, 64)]


def local(tokens, w_in, short_filter, mr_filter, skip, w_out, grad_out):
    vmem = pl.BlockSpec(memory_space=pltpu.VMEM)
    hbm = pl.BlockSpec(memory_space=pl.ANY)
    scratch = [
        pltpu.VMEM((64, ROWS), BF),
        pltpu.VMEM((64, ROWS), BF),
        pltpu.VMEM((3, 192), F32),
        pltpu.VMEM((4, TAPS), F32),
        pltpu.VMEM((1, 64), F32),
        pltpu.VMEM((192, 8192), BF),
        pltpu.VMEM((NP, 192, 256), BF),
        pltpu.VMEM((NZ, PAD, 128), BF),
        pltpu.VMEM((NP, PAD, 256), BF),
        pltpu.VMEM((256, 2048), BF),
        pltpu.VMEM((PAD, 192), F32),
        pltpu.VMEM((PAD, 256), BF),
        pltpu.VMEM((NX, PAD, 512), BF),
        pltpu.VMEM((NX, PAD, 512), BF),
        pltpu.VMEM((NY, CUT, 128), BF),
        pltpu.VMEM((NY, CUT, 128), BF),
        pltpu.VMEM((64, 128), BF),
        pltpu.VMEM((64, 128), BF),
        pltpu.VMEM((PAD, WIDE), BF),
        pltpu.VMEM((16, WIDE), BF),
        pltpu.VMEM((NP, CUT, 128), BF),
        pltpu.VMEM((NZ, CUT, 128), BF),
        pltpu.VMEM((NZ, CUT, 128), BF),
        pltpu.VMEM((NR, 8, 128), F32),
        pltpu.VMEM((4 * PAD, WIDE), BF),
        pltpu.SemaphoreType.DMA((NSEM,)),
        pltpu.SemaphoreType.DMA((NSEM,)),
        pltpu.SemaphoreType.DMA((7,)),
    ]
    sums = pl.pallas_call(
        kernel,
        out_shape=jax.ShapeDtypeStruct((PAD, 128), F32),
        in_specs=[hbm] * 7,
        out_specs=vmem,
        scratch_shapes=scratch,
        compiler_params=pltpu.CompilerParams(
            collective_id=0, has_side_effects=True, vmem_limit_bytes=56 * 1024 * 1024
        ),
        name="hyena_block",
    )(tokens.T, grad_out.T, w_in.T, short_filter, mr_filter, skip.reshape(1, 64), w_out.T)
    out, taps, gains = pl.pallas_call(
        split_results,
        out_shape=(
            jax.ShapeDtypeStruct((64, ROWS), BF),
            jax.ShapeDtypeStruct((4, TAPS), F32),
            jax.ShapeDtypeStruct((1, 64), F32),
        ),
        in_specs=[vmem],
        out_specs=(vmem, vmem, vmem),
        name="split_results",
    )(sums)
    return out.T, taps, gains.reshape(64)


def solution(mesh):
    in_specs = (
        P("row", "col"),
        P(None, "col"),
        P(None, "col"),
        P("col", None),
        P("col"),
        P(None, "col"),
        P("row", "col"),
    )
    out_specs = (P("row", "col"), P("col", None), P("col"))
    return jax.shard_map(local, mesh=mesh, in_specs=in_specs, out_specs=out_specs, check_vma=False)
```

```python
import jax
import jax.numpy as jnp
from jax import lax
from jax.experimental import pallas as pl
from jax.experimental.pallas import tpu as pltpu
from jax.sharding import PartitionSpec as P

MESH = pl.DeviceIdType.MESH
NX, NY, NZ, NR = 4, 8, 4, 6
NP = NX * NY
ROWS = 136
PAD = 144
CUT = 80
CUT2 = 64
TAPS = 128
WIDE = 384
BF = jnp.bfloat16
F32 = jnp.float32
HIGH = lax.Precision.HIGHEST
NSEM = 160


class Comm:
    def __init__(self, ss, rs):
        self.ss, self.rs, self.count, self.started = ss, rs, 0, []

    def send(self, src, dst, dev):
        i = self.count
        self.count += 1
        copy = pltpu.make_async_remote_copy(
            src_ref=src,
            dst_ref=dst,
            send_sem=self.ss.at[i],
            recv_sem=self.rs.at[i],
            device_id=dev,
            device_id_type=MESH,
        )
        copy.start()
        self.started.append(copy)
        return (i, dev)

    def arrive(self, handle, dst):
        i, dev = handle
        pltpu.make_async_remote_copy(
            src_ref=dst,
            dst_ref=dst,
            send_sem=self.ss.at[i],
            recv_sem=self.rs.at[i],
            device_id=dev,
            device_id_type=MESH,
        ).wait_recv()

    def finish(self):
        for copy in self.started:
            copy.wait_send()


def iota(shape, dim):
    return lax.broadcasted_iota(jnp.int32, shape, dim)


def swap(v):
    return pltpu.roll(v, 64, 1)


def low(v):
    return iota(v.shape, 1) < 64


def lows(a, b):
    return jnp.where(low(a), a, swap(b))


def highs(a, b):
    return jnp.where(low(a), swap(a), b)


def pack(tile, half):
    top = tile[:CUT]
    rest = jnp.concatenate([tile[CUT:], jnp.zeros((2 * CUT - PAD, 128), F32)], 0)
    return lows(top, rest) if half == 0 else highs(top, rest)


def unpack(v):
    up = swap(v)
    full = jnp.concatenate([v, up[: PAD - CUT]], 0)
    return jnp.where(low(full), full, 0.0)


def side_by_side(ref):
    q0, q1, q2, q3 = [ref[k].astype(F32) for k in range(4)]
    top = jnp.concatenate([lows(q0, q1), lows(q2, q3)], 1)
    rest = jnp.concatenate([highs(q0, q1), highs(q2, q3)], 1)[: PAD - CUT]
    return jnp.concatenate([top, rest], 0).astype(BF)


def dot(a, b):
    return jnp.dot(a, b, preferred_element_type=F32)


def dot_t(a, b):
    return lax.dot_general(a, b, (((1,), (1,)), ((), ())), preferred_element_type=F32)


def kernel(
    tok_in, grd_in, win, sfl_in, flt_in, skp_in, wout,
    res_ref,
    tok, grd, sfl, flt, skp, wraw, wv, zr, zg, gath, wz, acc, gz, gp, gr, yp, yr, hs, hr, pb, h2r, gated, op, orv, pr, toep,
    ss, rs, ls,
):
    r = lax.axis_index("row")
    c = lax.axis_index("col")
    core = r % 2
    z = c // NP
    x = (c // NY) % NX
    y = c % NY
    sgn = 1 - 2 * core
    comm = Comm(ss, rs)

    def at(dx=0, dy=0, dz=0):
        return (r, ((z + dz + NZ) % NZ) * NP + ((x + dx + NX) % NX) * NY + (y + dy + NY) % NY)

    def chunk(dx, dy):
        return ((x - dx + NX) % NX) * NY + (y - dy + NY) % NY

    def by_row(i):
        return ((r + i) % NR, c)

    sibling = (r + sgn, c)
    own = chunk(0, 0)

    peers = [at(dz=i) for i in range(1, NZ)] + [at(dx=i) for i in range(1, NX)]
    peers += [at(dy=i) for i in range(1, NY)] + [by_row(i) for i in range(1, NR)]
    barrier = pltpu.get_barrier_semaphore()
    for peer in peers:
        pl.semaphore_signal(barrier, inc=1, device_id=peer, device_id_type=MESH)

    mine = pl.multiple_of(z * 2048, 2048)
    keep = pl.multiple_of(z * 64, 64)
    pairs = [(tok_in, tok), (grd_in, grd), (sfl_in, sfl), (flt_in, flt), (skp_in, skp), (win, wraw)]
    pairs.append((wout.at[:, pl.ds(mine, 2048)], wz.at[pl.ds(keep, 64)]))
    loads = [pltpu.make_async_copy(a, b, ls.at[i]) for i, (a, b) in enumerate(pairs)]
    for load in loads:
        load.start()
    loads[0].wait()
    loads[1].wait()
    both = jnp.concatenate([tok[...].astype(F32), grd[...].astype(F32)], 0)
    both = jnp.concatenate([both, jnp.zeros((128, 256 - ROWS), F32)], 1)
    both = both.T[:PAD]
    zr[z] = pack(both, 0).astype(BF)
    zg[z] = pack(both, 1).astype(BF)

    pl.semaphore_wait(barrier, len(peers))

    z_moves = [comm.send(zr.at[z], zr.at[z], at(dz=i)) for i in (1, 2, 3)]

    col = iota((192, WIDE), 1)
    lane = col & 127
    source = (lane >> 4) * 48 + (col >> 7) * 16 + (lane & 15)
    hit = (iota((192, WIDE), 0) == source) & (lane < 64)
    perm = jnp.where(hit, 1.0, 0.0)
    loads[2].wait()
    loads[3].wait()
    short_taps = jnp.dot(sfl[...], perm, precision=HIGH, preferred_element_type=F32)
    perm_b = perm.astype(BF)

    place = jnp.where((iota((TAPS, WIDE), 0) + iota((TAPS, WIDE), 1)) % WIDE == 0, 1.0, 0.0).astype(BF)
    taps0 = dot(flt[...].astype(BF), place)
    for g in range(4):
        line = jnp.broadcast_to(taps0[g : g + 1], (PAD, WIDE))
        toep[pl.ds(g * PAD, PAD)] = pltpu.roll(line, 0, 1, stride=1, stride_axis=0).astype(BF)

    loads[5].wait()

    def reorder(pair, carry):
        tiles = [wraw[:, pl.ds(pl.multiple_of(k * 2048 + pair * 128, 128), 128)] for k in range(NZ)]
        t0, t1, t2, t3 = [v.astype(F32) for v in tiles]
        wv[2 * pair] = jnp.concatenate([lows(t0, t1), lows(t2, t3)], 1).astype(BF)
        wv[2 * pair + 1] = jnp.concatenate([highs(t0, t1), highs(t2, t3)], 1).astype(BF)
        return carry

    lax.fori_loop(0, NP // 2, reorder, 0)
    for i, move in zip((1, 2, 3), z_moves):
        comm.arrive(move, zr.at[(z - i + NZ) % NZ])
    g_moves = [comm.send(zg.at[z], zg.at[z], at(dz=i)) for i in (1, 2, 3)]

    half = pl.multiple_of(core * 1024, 1024)
    w_moves = []
    for i in (1, 2, 3):
        base = pl.multiple_of(((z + i) % NZ) * 2048 + core * 1024, 1024)
        w_moves.append(
            comm.send(wout.at[:, pl.ds(base, 1024)], wz.at[pl.ds(keep, 64), pl.ds(half, 1024)], at(dz=i))
        )

    gath[own] = side_by_side(zr)

    parts = {"A": pl.ds(0, CUT), "B": pl.ds(CUT, PAD - CUT)}
    moves = {}

    def pass_on(part, dx, dy, to_dx, to_dy, step_x, step_y):
        ref = gath.at[chunk(dx, dy), parts[part]]
        moves[part, to_dx, to_dy] = comm.send(ref, ref, at(dx=step_x, dy=step_y))

    def y_steps(part, dx, dy):
        if 0 <= dy <= 2:
            pass_on(part, dx, dy, dx, dy + 1, 0, 1)
        if -2 <= dy <= 0:
            pass_on(part, dx, dy, dx, dy - 1, 0, -1)
        if dy == -3:
            pass_on(part, dx, 3 * sgn, dx, 4, 0, sgn)

    def x_steps(part, dx, dy):
        if dx == 0:
            pass_on(part, 0, dy, 1, dy, 1, 0)
            pass_on(part, 0, dy, -1, dy, -1, 0)
            pass_on(part, 0, dy, 2, dy, 2, 0)

    def forward(part, dx, dy):
        if part == "A":
            if dx == 0:
                y_steps(part, 0, dy)
            x_steps(part, dx, dy)
        else:
            if dy == 0:
                x_steps(part, dx, 0)
            y_steps(part, dx, dy)

    def hops(d):
        return min(abs(d[0]), 1) + abs(d[1])

    order = sorted(
        [(dx, dy) for dx in (0, 1, -1, 2) for dy in (0, 1, -1, 2, -2, 3, -3, 4)],
        key=lambda d: (hops(d), abs(d[0]), -d[0], -d[1]),
    )
    forward("A", 0, 0)
    forward("B", 0, 0)

    def project(places):
        total = None
        for dx, dy in places:
            p = chunk(dx, dy)
            term = dot_t(gath[p], wv[p])
            total = term if total is None else total + term
        return total

    acc[...] = project([(0, 0)])
    w_back = []
    gx_moves = []

    def sum_over_x():
        loads[6].wait()
        other = pl.multiple_of(1024 - core * 1024, 1024)
        for i, move in zip((1, 2, 3), w_back):
            comm.arrive(move, wz.at[pl.ds(pl.multiple_of(((z - i + NZ) % NZ) * 64, 64), 64), pl.ds(other, 1024)])
        for i, move in zip((1, 2, 3), g_moves):
            comm.arrive(move, zg.at[(z - i + NZ) % NZ])
        gz[...] = side_by_side(zg)
        for k in range(NX):
            gp[k] = dot(gz[...], wz[:, pl.ds(512 * k, 512)]).astype(BF)
        for i in (1, 3, 2):
            gx_moves.append(comm.send(gp.at[(x + i) % NX], gr.at[x], at(dx=i)))

    for hop in range(1, 6):
        places = [d for d in order if hops(d) == hop]
        for dx, dy in places:
            for part in ("A", "B"):
                comm.arrive(moves[part, dx, dy], gath.at[chunk(dx, dy), parts[part]])
                forward(part, dx, dy)
        if hop == 3:
            for i, move in zip((1, 2, 3), w_moves):
                ref = wz.at[pl.ds(pl.multiple_of(((z - i + NZ) % NZ) * 64, 64), 64), pl.ds(half, 1024)]
                comm.arrive(move, ref)
                w_back.append(comm.send(ref, ref, sibling))
        if hop == 4:
            sum_over_x()
        acc[...] += project(places)

    proj = dot(acc[...].astype(BF), perm_b)
    pb[...] = proj.astype(BF)
    tail_move = comm.send(pb.at[pl.ds(128, 16)], h2r, by_row(1))
    t = iota((PAD, WIDE), 0)
    one = jnp.where(t >= 1, pltpu.roll(proj, 1, 0), 0.0)
    two = jnp.where(t >= 2, pltpu.roll(proj, 2, 0), 0.0)
    s0, s1, s2 = short_taps[0:1], short_taps[1:2], short_taps[2:3]
    short = s0 * proj + s1 * one + s2 * two
    live = iota((PAD, 128), 0) < ROWS
    mixed = jnp.where(live, short[:, 128:256] * short[:, 256:384], 0.0)
    hs[...] = lows(mixed[8:72], mixed[72:136]).astype(BF)
    halo_move = comm.send(hs, hr, by_row(1))

    comm.arrive(tail_move, h2r)
    last = jnp.where(r > 0, h2r[...].astype(F32), 0.0)
    before1, before2 = last[7:8], last[6:7]
    t8 = iota((8, WIDE), 0)
    fix = jnp.where(t8 == 0, s1 * before1 + s2 * before2, jnp.where(t8 == 1, s2 * before1, 0.0))
    short = jnp.concatenate([short[:8] + fix, short[8:]], 0)
    query = short[:, :128]
    mixed = jnp.where(live, short[:, 128:256] * short[:, 256:384], 0.0)
    own_b = jnp.concatenate([mixed, jnp.zeros((256 - PAD, 128), F32)], 0).astype(BF)
    near = dot(toep[:, :256], own_b)
    comm.arrive(halo_move, hr)
    h = jnp.where(r > 0, hr[...].astype(F32), 0.0)
    prev = jnp.concatenate([jnp.where(low(h), h, 0.0), jnp.where(low(h), swap(h), 0.0)], 0)
    prev_b = prev.astype(BF)
    big = near + dot(toep[:, 256:], prev_b)
    group = iota((PAD, 128), 1) >> 4
    conv = jnp.zeros((PAD, 128), F32)
    for g in range(4):
        conv = jnp.where(group == g, big[g * PAD : (g + 1) * PAD], conv)
    loads[4].wait()
    skip = jnp.concatenate([skp[...], jnp.zeros((1, 64), F32)], 1)
    value = query * (conv + skip * mixed)
    gated[own] = pack(value, 0).astype(BF)

    parts2 = {"A": pl.ds(0, CUT2), "B": pl.ds(CUT2, CUT - CUT2)}
    moves2 = {}
    ys, xs = (1, 7, 2, 6, 3, 5, 4), (1, 3, 2)

    def direct(part, dx, dy, step_x, step_y):
        ref = gated.at[chunk(dx, dy), parts2[part]]
        moves2[part, dx + step_x, dy + step_y] = comm.send(ref, ref, at(dx=step_x, dy=step_y))

    for dy in ys:
        direct("A", 0, 0, 0, dy)
    for dx in xs:
        direct("B", 0, 0, dx, 0)
        direct("A", 0, 0, dx, 0)
    for dy in ys:
        direct("B", 0, 0, 0, dy)

    total = gp[x].astype(F32)
    for i, move in zip((1, 3, 2), gx_moves):
        comm.arrive(move, gr.at[(x - i + NX) % NX])
        total = total + gr[(x - i + NX) % NX].astype(F32)
    for k in range(NY):
        yp[k] = pack(total[:, 128 * (k // 2) : 128 * (k // 2) + 128], k % 2).astype(BF)

    for dx in xs:
        comm.arrive(moves2["B", dx, 0], gated.at[chunk(dx, 0), parts2["B"]])
        for dy in ys:
            direct("B", dx, 0, 0, dy)
    for dy in ys:
        comm.arrive(moves2["A", 0, dy], gated.at[chunk(0, dy), parts2["A"]])
        for dx in xs:
            direct("A", 0, dy, dx, 0)
    gy_moves = [comm.send(yp.at[(y + i) % NY], yr.at[y], at(dy=i)) for i in ys]

    grad = unpack(yp[y].astype(F32))
    for i, move in zip(ys, gy_moves):
        comm.arrive(move, yr.at[(y - i + NY) % NY])
        grad = grad + unpack(yr[(y - i + NY) % NY].astype(F32))
    weighted = jnp.where(live, grad * query, 0.0)
    skip_part = jnp.sum(weighted * mixed, axis=0, keepdims=True)
    flip = jnp.where(iota((PAD, PAD), 0) + iota((PAD, PAD), 1) == PAD - 1, 1.0, 0.0).astype(BF)
    back = dot(flip, weighted.astype(BF))
    stack = jnp.concatenate([jnp.where(group == g, back, 0.0) for g in range(4)], 0).astype(BF)
    ext = jnp.concatenate([own_b, prev_b], 0)
    corr = dot_t(stack, ext)
    lines = [
        jnp.sum(
            pltpu.roll(corr[g * PAD : (g + 1) * PAD], 0, 1, stride=1, stride_axis=0), axis=0, keepdims=True
        )
        for g in range(4)
    ]
    lines = jnp.concatenate(lines + [jnp.zeros((4, WIDE), F32)], 0)
    pick = jnp.where(iota((WIDE, TAPS), 0) + iota((WIDE, TAPS), 1) == PAD - 1, 1.0, 0.0)
    tap_part = jnp.dot(lines, pick, precision=HIGH, preferred_element_type=F32)
    pr[r] = jnp.where(iota((8, 128), 0) == 4, skip_part, tap_part)
    row_moves = [comm.send(pr.at[r], pr.at[r], by_row(i)) for i in range(1, NR)]

    for dx in xs:
        comm.arrive(moves2["A", dx, 0], gated.at[chunk(dx, 0), parts2["A"]])
    for dy in ys:
        comm.arrive(moves2["B", 0, dy], gated.at[chunk(0, dy), parts2["B"]])
    for dy in ys:
        for dx in xs:
            for part in ("A", "B"):
                comm.arrive(moves2[part, dx, dy], gated.at[chunk(dx, dy), parts2[part]])
    outp = jnp.zeros((PAD, 256), F32)
    for k in range(NP // 4):
        u0, u1, u2, u3 = [gated[4 * k + i].astype(F32) for i in range(4)]
        top = jnp.concatenate([lows(u0, u1), lows(u2, u3)], 1)
        rest = jnp.concatenate([highs(u0, u1), highs(u2, u3)], 1)[: PAD - CUT]
        outp = outp + dot_t(jnp.concatenate([top, rest], 0).astype(BF), wz[:, pl.ds(256 * k, 256)])
    for k in range(NZ):
        op[k] = pack(outp[:, 128 * (k // 2) : 128 * (k // 2) + 128], k % 2).astype(BF)
    o_moves = [comm.send(op.at[(z + i) % NZ], orv.at[z], at(dz=i)) for i in (1, 2, 3)]
    result = op[z].astype(F32)
    for i, move in zip((1, 2, 3), o_moves):
        comm.arrive(move, orv.at[(z - i + NZ) % NZ])
        result = result + orv[(z - i + NZ) % NZ].astype(F32)
    res_ref[pl.ds(0, ROWS)] = unpack(result)[:ROWS]

    for i, move in zip(range(1, NR), row_moves):
        comm.arrive(move, pr.at[(r - i + NR) % NR])
    sums = pr[0]
    for k in range(1, NR):
        sums = sums + pr[k]
    res_ref[pl.ds(ROWS, 8)] = sums
    comm.finish()
    assert comm.count <= NSEM


def split_results(res_ref, out_ref, fg_ref, sg_ref):
    block = jnp.concatenate([res_ref[pl.ds(0, ROWS)], jnp.zeros((256 - ROWS, 128), F32)], 0)
    out_ref[...] = block.T[:64, :ROWS].astype(BF)
    fg_ref[...] = res_ref[pl.ds(ROWS, 4)]
    sg_ref[...] = res_ref[pl.ds(ROWS + 4, 1), pl.ds(0, 64)]


def local(tokens, w_in, short_filter, mr_filter, skip, w_out, grad_out):
    vmem = pl.BlockSpec(memory_space=pltpu.VMEM)
    hbm = pl.BlockSpec(memory_space=pl.ANY)
    scratch = [
        pltpu.VMEM((64, ROWS), BF),
        pltpu.VMEM((64, ROWS), BF),
        pltpu.VMEM((3, 192), F32),
        pltpu.VMEM((4, TAPS), F32),
        pltpu.VMEM((1, 64), F32),
        pltpu.VMEM((192, 8192), BF),
        pltpu.VMEM((NP, 192, 256), BF),
        pltpu.VMEM((NZ, CUT, 128), BF),
        pltpu.VMEM((NZ, CUT, 128), BF),
        pltpu.VMEM((NP, PAD, 256), BF),
        pltpu.VMEM((256, 2048), BF),
        pltpu.VMEM((PAD, 192), F32),
        pltpu.VMEM((PAD, 256), BF),
        pltpu.VMEM((NX, PAD, 512), BF),
        pltpu.VMEM((NX, PAD, 512), BF),
        pltpu.VMEM((NY, CUT, 128), BF),
        pltpu.VMEM((NY, CUT, 128), BF),
        pltpu.VMEM((64, 128), BF),
        pltpu.VMEM((64, 128), BF),
        pltpu.VMEM((PAD, WIDE), BF),
        pltpu.VMEM((16, WIDE), BF),
        pltpu.VMEM((NP, CUT, 128), BF),
        pltpu.VMEM((NZ, CUT, 128), BF),
        pltpu.VMEM((NZ, CUT, 128), BF),
        pltpu.VMEM((NR, 8, 128), F32),
        pltpu.VMEM((4 * PAD, WIDE), BF),
        pltpu.SemaphoreType.DMA((NSEM,)),
        pltpu.SemaphoreType.DMA((NSEM,)),
        pltpu.SemaphoreType.DMA((7,)),
    ]
    sums = pl.pallas_call(
        kernel,
        out_shape=jax.ShapeDtypeStruct((PAD, 128), F32),
        in_specs=[hbm] * 7,
        out_specs=vmem,
        scratch_shapes=scratch,
        compiler_params=pltpu.CompilerParams(
            collective_id=0, has_side_effects=True, vmem_limit_bytes=56 * 1024 * 1024
        ),
        name="hyena_block",
    )(tokens.T, grad_out.T, w_in.T, short_filter, mr_filter, skip.reshape(1, 64), w_out.T)
    out, taps, gains = pl.pallas_call(
        split_results,
        out_shape=(
            jax.ShapeDtypeStruct((64, ROWS), BF),
            jax.ShapeDtypeStruct((4, TAPS), F32),
            jax.ShapeDtypeStruct((1, 64), F32),
        ),
        in_specs=[vmem],
        out_specs=(vmem, vmem, vmem),
        name="split_results",
    )(sums)
    return out.T, taps, gains.reshape(64)


def solution(mesh):
    in_specs = (
        P("row", "col"),
        P(None, "col"),
        P(None, "col"),
        P("col", None),
        P("col"),
        P(None, "col"),
        P("row", "col"),
    )
    out_specs = (P("row", "col"), P("col", None), P("col"))
    return jax.shard_map(local, mesh=mesh, in_specs=in_specs, out_specs=out_specs, check_vma=False)
```

```python
import jax
import jax.numpy as jnp
from jax import lax
from jax.experimental import pallas as pl
from jax.experimental.pallas import tpu as pltpu
from jax.sharding import PartitionSpec as P

MESH = pl.DeviceIdType.MESH
NX, NY, NZ, NR = 4, 8, 4, 6
NP = NX * NY
ROWS = 136
PAD = 144
CUT = 80
CUT2 = 64
REST = ROWS - CUT
TAPS = 128
WIDE = 384
BF = jnp.bfloat16
F32 = jnp.float32
HIGH = lax.Precision.HIGHEST
NSEM = 160


class Comm:
    def __init__(self, ss, rs):
        self.ss, self.rs, self.count, self.started = ss, rs, 0, []

    def send(self, src, dst, dev):
        i = self.count
        self.count += 1
        copy = pltpu.make_async_remote_copy(
            src_ref=src,
            dst_ref=dst,
            send_sem=self.ss.at[i],
            recv_sem=self.rs.at[i],
            device_id=dev,
            device_id_type=MESH,
        )
        copy.start()
        self.started.append(copy)
        return (i, dev)

    def arrive(self, handle, dst):
        i, dev = handle
        pltpu.make_async_remote_copy(
            src_ref=dst,
            dst_ref=dst,
            send_sem=self.ss.at[i],
            recv_sem=self.rs.at[i],
            device_id=dev,
            device_id_type=MESH,
        ).wait_recv()

    def finish(self):
        for copy in self.started:
            copy.wait_send()


def iota(shape, dim):
    return lax.broadcasted_iota(jnp.int32, shape, dim)


def swap(v):
    return pltpu.roll(v, 64, 1)


def low(v):
    return iota(v.shape, 1) < 64


def lows(a, b):
    return jnp.where(low(a), a, swap(b))


def highs(a, b):
    return jnp.where(low(a), swap(a), b)


def pack(tile, half):
    top = tile[:CUT]
    rest = jnp.concatenate([tile[CUT:], jnp.zeros((2 * CUT - PAD, 128), F32)], 0)
    return lows(top, rest) if half == 0 else highs(top, rest)


def unpack(v):
    up = swap(v)
    full = jnp.concatenate([v, up[: PAD - CUT]], 0)
    return jnp.where(low(full), full, 0.0)


def side_by_side(ref):
    q0, q1, q2, q3 = [ref[k].astype(F32) for k in range(4)]
    top = jnp.concatenate([lows(q0, q1), lows(q2, q3)], 1)
    rest = jnp.concatenate([highs(q0, q1), highs(q2, q3)], 1)[: PAD - CUT]
    return jnp.concatenate([top, rest], 0)


def dot(a, b):
    return jnp.dot(a, b, preferred_element_type=F32)


def dot_t(a, b):
    return lax.dot_general(a, b, (((1,), (1,)), ((), ())), preferred_element_type=F32)


def kernel(
    tok_in, grd_in, win, sfl_in, flt_in, skp_in, wout,
    res_ref,
    tok, grd, sfl, flt, skp, wraw, wv, zr, zg, gath_a, gath_b, wz, acc, gz, gp, gr, yp, yr, hs, hr, pb, h2r, gated, op, orv, pr, toep,
    ss, rs, ls,
):
    r = lax.axis_index("row")
    c = lax.axis_index("col")
    core = r % 2
    z = c // NP
    x = (c // NY) % NX
    y = c % NY
    sgn = 1 - 2 * core
    comm = Comm(ss, rs)

    def at(dx=0, dy=0, dz=0):
        return (r, ((z + dz + NZ) % NZ) * NP + ((x + dx + NX) % NX) * NY + (y + dy + NY) % NY)

    def chunk(dx, dy):
        return ((x - dx + NX) % NX) * NY + (y - dy + NY) % NY

    def by_row(i):
        return ((r + i) % NR, c)

    sibling = (r + sgn, c)
    own = chunk(0, 0)

    peers = [at(dz=i) for i in range(1, NZ)] + [at(dx=i) for i in range(1, NX)]
    peers += [at(dy=i) for i in range(1, NY)] + [by_row(i) for i in range(1, NR)]
    barrier = pltpu.get_barrier_semaphore()
    for peer in peers:
        pl.semaphore_signal(barrier, inc=1, device_id=peer, device_id_type=MESH)

    mine = pl.multiple_of(z * 2048, 2048)
    keep = pl.multiple_of(z * 64, 64)
    pairs = [(tok_in, tok), (grd_in, grd), (sfl_in, sfl), (flt_in, flt), (skp_in, skp), (win, wraw)]
    pairs.append((wout.at[:, pl.ds(mine, 2048)], wz.at[pl.ds(keep, 64)]))
    loads = [pltpu.make_async_copy(a, b, ls.at[i]) for i, (a, b) in enumerate(pairs)]
    for load in loads:
        load.start()
    loads[0].wait()
    loads[1].wait()
    both = jnp.concatenate([tok[...].astype(F32), grd[...].astype(F32)], 0)
    both = jnp.concatenate([both, jnp.zeros((128, 256 - ROWS), F32)], 1)
    both = both.T[:PAD]
    zr[z] = pack(both, 0).astype(BF)
    zg[z] = pack(both, 1).astype(BF)

    pl.semaphore_wait(barrier, len(peers))

    z_moves = [comm.send(zr.at[z], zr.at[z], at(dz=i)) for i in (1, 2, 3)]

    col = iota((192, WIDE), 1)
    lane = col & 127
    source = (lane >> 4) * 48 + (col >> 7) * 16 + (lane & 15)
    hit = (iota((192, WIDE), 0) == source) & (lane < 64)
    perm = jnp.where(hit, 1.0, 0.0)
    loads[2].wait()
    loads[3].wait()
    short_taps = jnp.dot(sfl[...], perm, precision=HIGH, preferred_element_type=F32)
    perm_b = perm.astype(BF)

    place = jnp.where((iota((TAPS, WIDE), 0) + iota((TAPS, WIDE), 1)) % WIDE == 0, 1.0, 0.0).astype(BF)
    taps0 = dot(flt[...].astype(BF), place)
    for g in range(4):
        line = jnp.broadcast_to(taps0[g : g + 1], (PAD, WIDE))
        toep[pl.ds(g * PAD, PAD)] = pltpu.roll(line, 0, 1, stride=1, stride_axis=0).astype(BF)

    loads[5].wait()

    def reorder(pair, carry):
        tiles = [wraw[:, pl.ds(pl.multiple_of(k * 2048 + pair * 128, 128), 128)] for k in range(NZ)]
        t0, t1, t2, t3 = [v.astype(F32) for v in tiles]
        wv[2 * pair] = jnp.concatenate([lows(t0, t1), lows(t2, t3)], 1).astype(BF)
        wv[2 * pair + 1] = jnp.concatenate([highs(t0, t1), highs(t2, t3)], 1).astype(BF)
        return carry

    lax.fori_loop(0, NP // 2, reorder, 0)
    for i, move in zip((1, 2, 3), z_moves):
        comm.arrive(move, zr.at[(z - i + NZ) % NZ])
    g_moves = [comm.send(zg.at[z], zg.at[z], at(dz=i)) for i in (1, 2, 3)]

    half = pl.multiple_of(core * 1024, 1024)
    w_moves = []
    for i in (1, 2, 3):
        base = pl.multiple_of(((z + i) % NZ) * 2048 + core * 1024, 1024)
        w_moves.append(
            comm.send(wout.at[:, pl.ds(base, 1024)], wz.at[pl.ds(keep, 64), pl.ds(half, 1024)], at(dz=i))
        )

    mine_all = side_by_side(zr)
    gath_a[own] = mine_all[:CUT].astype(BF)
    gath_b[own] = jnp.concatenate([mine_all[CUT:ROWS, :128], mine_all[CUT:ROWS, 128:]], 0).astype(BF)

    parts = {"A": gath_a, "B": gath_b}
    moves = {}

    def pass_on(part, dx, dy, to_dx, to_dy, step_x, step_y):
        ref = parts[part].at[chunk(dx, dy)]
        moves[part, to_dx, to_dy] = comm.send(ref, ref, at(dx=step_x, dy=step_y))

    def y_steps(part, dx, dy):
        if 0 <= dy <= 2:
            pass_on(part, dx, dy, dx, dy + 1, 0, 1)
        if -2 <= dy <= 0:
            pass_on(part, dx, dy, dx, dy - 1, 0, -1)
        if dy == -3:
            pass_on(part, dx, 3 * sgn, dx, 4, 0, sgn)

    def x_steps(part, dx, dy):
        if dx == 0:
            pass_on(part, 0, dy, 1, dy, 1, 0)
            pass_on(part, 0, dy, -1, dy, -1, 0)
            pass_on(part, 0, dy, 2, dy, 2, 0)

    def forward(part, dx, dy):
        if part == "A":
            if dx == 0:
                y_steps(part, 0, dy)
            x_steps(part, dx, dy)
        else:
            if dy == 0:
                x_steps(part, dx, 0)
            y_steps(part, dx, dy)

    def hops(d):
        return min(abs(d[0]), 1) + abs(d[1])

    order = sorted(
        [(dx, dy) for dx in (0, 1, -1, 2) for dy in (0, 1, -1, 2, -2, 3, -3, 4)],
        key=lambda d: (hops(d), abs(d[0]), -d[0], -d[1]),
    )
    forward("A", 0, 0)
    forward("B", 0, 0)

    def project(places):
        total = None
        for dx, dy in places:
            p = chunk(dx, dy)
            w, b = wv[p], gath_b[p]
            term = jnp.concatenate([dot_t(gath_a[p], w), dot_t(b, w[:, :128]), dot_t(b, w[:, 128:])], 0)
            total = term if total is None else total + term
        return total

    acc[...] = project([(0, 0)])
    w_back = []
    gx_moves = []

    def sum_over_x():
        loads[6].wait()
        other = pl.multiple_of(1024 - core * 1024, 1024)
        for i, move in zip((1, 2, 3), w_back):
            comm.arrive(move, wz.at[pl.ds(pl.multiple_of(((z - i + NZ) % NZ) * 64, 64), 64), pl.ds(other, 1024)])
        for i, move in zip((1, 2, 3), g_moves):
            comm.arrive(move, zg.at[(z - i + NZ) % NZ])
        gz[...] = side_by_side(zg).astype(BF)
        for k in range(NX):
            gp[k] = dot(gz[...], wz[:, pl.ds(512 * k, 512)]).astype(BF)
        for i in (1, 3, 2):
            gx_moves.append(comm.send(gp.at[(x + i) % NX], gr.at[x], at(dx=i)))

    for hop in range(1, 6):
        places = [d for d in order if hops(d) == hop]
        for dx, dy in places:
            for part in ("A", "B"):
                comm.arrive(moves[part, dx, dy], parts[part].at[chunk(dx, dy)])
                forward(part, dx, dy)
        if hop == 3:
            for i, move in zip((1, 2, 3), w_moves):
                ref = wz.at[pl.ds(pl.multiple_of(((z - i + NZ) % NZ) * 64, 64), 64), pl.ds(half, 1024)]
                comm.arrive(move, ref)
                w_back.append(comm.send(ref, ref, sibling))
        if hop == 4:
            sum_over_x()
        acc[...] += project(places)

    rest = acc[pl.ds(CUT, REST)] + acc[pl.ds(CUT + 3 * REST, REST)]
    whole = jnp.concatenate([acc[pl.ds(0, CUT)], rest, jnp.zeros((PAD - ROWS, 192), F32)], 0)
    proj = dot(whole.astype(BF), perm_b)
    pb[...] = proj.astype(BF)
    tail_move = comm.send(pb.at[pl.ds(128, 16)], h2r, by_row(1))
    t = iota((PAD, WIDE), 0)
    one = jnp.where(t >= 1, pltpu.roll(proj, 1, 0), 0.0)
    two = jnp.where(t >= 2, pltpu.roll(proj, 2, 0), 0.0)
    s0, s1, s2 = short_taps[0:1], short_taps[1:2], short_taps[2:3]
    short = s0 * proj + s1 * one + s2 * two
    live = iota((PAD, 128), 0) < ROWS
    mixed = jnp.where(live, short[:, 128:256] * short[:, 256:384], 0.0)
    hs[...] = lows(mixed[8:72], mixed[72:136]).astype(BF)
    halo_move = comm.send(hs, hr, by_row(1))

    comm.arrive(tail_move, h2r)
    last = jnp.where(r > 0, h2r[...].astype(F32), 0.0)
    before1, before2 = last[7:8], last[6:7]
    t8 = iota((8, WIDE), 0)
    fix = jnp.where(t8 == 0, s1 * before1 + s2 * before2, jnp.where(t8 == 1, s2 * before1, 0.0))
    short = jnp.concatenate([short[:8] + fix, short[8:]], 0)
    query = short[:, :128]
    mixed = jnp.where(live, short[:, 128:256] * short[:, 256:384], 0.0)
    own_b = jnp.concatenate([mixed, jnp.zeros((256 - PAD, 128), F32)], 0).astype(BF)
    near = dot(toep[:, :256], own_b)
    comm.arrive(halo_move, hr)
    h = jnp.where(r > 0, hr[...].astype(F32), 0.0)
    prev = jnp.concatenate([jnp.where(low(h), h, 0.0), jnp.where(low(h), swap(h), 0.0)], 0)
    prev_b = prev.astype(BF)
    big = near + dot(toep[:, 256:], prev_b)
    group = iota((PAD, 128), 1) >> 4
    conv = jnp.zeros((PAD, 128), F32)
    for g in range(4):
        conv = jnp.where(group == g, big[g * PAD : (g + 1) * PAD], conv)
    loads[4].wait()
    skip = jnp.concatenate([skp[...], jnp.zeros((1, 64), F32)], 1)
    value = query * (conv + skip * mixed)
    gated[own] = pack(value, 0).astype(BF)

    parts2 = {"A": pl.ds(0, CUT2), "B": pl.ds(CUT2, CUT - CUT2)}
    moves2 = {}
    ys, xs = (1, 7, 2, 6, 3, 5, 4), (1, 3, 2)

    def direct(part, dx, dy, step_x, step_y):
        ref = gated.at[chunk(dx, dy), parts2[part]]
        moves2[part, dx + step_x, dy + step_y] = comm.send(ref, ref, at(dx=step_x, dy=step_y))

    for dy in ys:
        direct("A", 0, 0, 0, dy)
    for dx in xs:
        direct("B", 0, 0, dx, 0)
        direct("A", 0, 0, dx, 0)
    for dy in ys:
        direct("B", 0, 0, 0, dy)

    total = gp[x].astype(F32)
    for i, move in zip((1, 3, 2), gx_moves):
        comm.arrive(move, gr.at[(x - i + NX) % NX])
        total = total + gr[(x - i + NX) % NX].astype(F32)
    for k in range(NY):
        yp[k] = pack(total[:, 128 * (k // 2) : 128 * (k // 2) + 128], k % 2).astype(BF)

    for dx in xs:
        comm.arrive(moves2["B", dx, 0], gated.at[chunk(dx, 0), parts2["B"]])
        for dy in ys:
            direct("B", dx, 0, 0, dy)
    for dy in ys:
        comm.arrive(moves2["A", 0, dy], gated.at[chunk(0, dy), parts2["A"]])
        for dx in xs:
            direct("A", 0, dy, dx, 0)
    gy_moves = [comm.send(yp.at[(y + i) % NY], yr.at[y], at(dy=i)) for i in ys]

    grad = unpack(yp[y].astype(F32))
    for i, move in zip(ys, gy_moves):
        comm.arrive(move, yr.at[(y - i + NY) % NY])
        grad = grad + unpack(yr[(y - i + NY) % NY].astype(F32))
    weighted = jnp.where(live, grad * query, 0.0)
    skip_part = jnp.sum(weighted * mixed, axis=0, keepdims=True)
    flip = jnp.where(iota((PAD, PAD), 0) + iota((PAD, PAD), 1) == PAD - 1, 1.0, 0.0).astype(BF)
    back = dot(flip, weighted.astype(BF))
    stack = jnp.concatenate([jnp.where(group == g, back, 0.0) for g in range(4)], 0).astype(BF)
    ext = jnp.concatenate([own_b, prev_b], 0)
    corr = dot_t(stack, ext)
    lines = [
        jnp.sum(
            pltpu.roll(corr[g * PAD : (g + 1) * PAD], 0, 1, stride=1, stride_axis=0), axis=0, keepdims=True
        )
        for g in range(4)
    ]
    lines = jnp.concatenate(lines + [jnp.zeros((4, WIDE), F32)], 0)
    pick = jnp.where(iota((WIDE, TAPS), 0) + iota((WIDE, TAPS), 1) == PAD - 1, 1.0, 0.0)
    tap_part = jnp.dot(lines, pick, precision=HIGH, preferred_element_type=F32)
    pr[r] = jnp.where(iota((8, 128), 0) == 4, skip_part, tap_part)
    row_moves = [comm.send(pr.at[r], pr.at[r], by_row(i)) for i in range(1, NR)]

    for dx in xs:
        comm.arrive(moves2["A", dx, 0], gated.at[chunk(dx, 0), parts2["A"]])
    for dy in ys:
        comm.arrive(moves2["B", 0, dy], gated.at[chunk(0, dy), parts2["B"]])
    for dy in ys:
        for dx in xs:
            for part in ("A", "B"):
                comm.arrive(moves2[part, dx, dy], gated.at[chunk(dx, dy), parts2[part]])
    outp = jnp.zeros((PAD, 256), F32)
    for k in range(NP // 4):
        u0, u1, u2, u3 = [gated[4 * k + i].astype(F32) for i in range(4)]
        top = jnp.concatenate([lows(u0, u1), lows(u2, u3)], 1)
        rest = jnp.concatenate([highs(u0, u1), highs(u2, u3)], 1)[: PAD - CUT]
        outp = outp + dot_t(jnp.concatenate([top, rest], 0).astype(BF), wz[:, pl.ds(256 * k, 256)])
    for k in range(NZ):
        op[k] = pack(outp[:, 128 * (k // 2) : 128 * (k // 2) + 128], k % 2).astype(BF)
    o_moves = [comm.send(op.at[(z + i) % NZ], orv.at[z], at(dz=i)) for i in (1, 2, 3)]
    result = op[z].astype(F32)
    for i, move in zip((1, 2, 3), o_moves):
        comm.arrive(move, orv.at[(z - i + NZ) % NZ])
        result = result + orv[(z - i + NZ) % NZ].astype(F32)
    res_ref[pl.ds(0, ROWS)] = unpack(result)[:ROWS]

    for i, move in zip(range(1, NR), row_moves):
        comm.arrive(move, pr.at[(r - i + NR) % NR])
    sums = pr[0]
    for k in range(1, NR):
        sums = sums + pr[k]
    res_ref[pl.ds(ROWS, 8)] = sums
    comm.finish()
    assert comm.count <= NSEM


def split_results(res_ref, out_ref, fg_ref, sg_ref):
    block = jnp.concatenate([res_ref[pl.ds(0, ROWS)], jnp.zeros((256 - ROWS, 128), F32)], 0)
    out_ref[...] = block.T[:64, :ROWS].astype(BF)
    fg_ref[...] = res_ref[pl.ds(ROWS, 4)]
    sg_ref[...] = res_ref[pl.ds(ROWS + 4, 1), pl.ds(0, 64)]


def local(tokens, w_in, short_filter, mr_filter, skip, w_out, grad_out):
    vmem = pl.BlockSpec(memory_space=pltpu.VMEM)
    hbm = pl.BlockSpec(memory_space=pl.ANY)
    scratch = [
        pltpu.VMEM((64, ROWS), BF),
        pltpu.VMEM((64, ROWS), BF),
        pltpu.VMEM((3, 192), F32),
        pltpu.VMEM((4, TAPS), F32),
        pltpu.VMEM((1, 64), F32),
        pltpu.VMEM((192, 8192), BF),
        pltpu.VMEM((NP, 192, 256), BF),
        pltpu.VMEM((NZ, CUT, 128), BF),
        pltpu.VMEM((NZ, CUT, 128), BF),
        pltpu.VMEM((NP, CUT, 256), BF),
        pltpu.VMEM((NP, 2 * REST, 128), BF),
        pltpu.VMEM((256, 2048), BF),
        pltpu.VMEM((CUT + 4 * REST, 192), F32),
        pltpu.VMEM((PAD, 256), BF),
        pltpu.VMEM((NX, PAD, 512), BF),
        pltpu.VMEM((NX, PAD, 512), BF),
        pltpu.VMEM((NY, CUT, 128), BF),
        pltpu.VMEM((NY, CUT, 128), BF),
        pltpu.VMEM((64, 128), BF),
        pltpu.VMEM((64, 128), BF),
        pltpu.VMEM((PAD, WIDE), BF),
        pltpu.VMEM((16, WIDE), BF),
        pltpu.VMEM((NP, CUT, 128), BF),
        pltpu.VMEM((NZ, CUT, 128), BF),
        pltpu.VMEM((NZ, CUT, 128), BF),
        pltpu.VMEM((NR, 8, 128), F32),
        pltpu.VMEM((4 * PAD, WIDE), BF),
        pltpu.SemaphoreType.DMA((NSEM,)),
        pltpu.SemaphoreType.DMA((NSEM,)),
        pltpu.SemaphoreType.DMA((7,)),
    ]
    sums = pl.pallas_call(
        kernel,
        out_shape=jax.ShapeDtypeStruct((PAD, 128), F32),
        in_specs=[hbm] * 7,
        out_specs=vmem,
        scratch_shapes=scratch,
        compiler_params=pltpu.CompilerParams(
            collective_id=0, has_side_effects=True, vmem_limit_bytes=56 * 1024 * 1024
        ),
        name="hyena_block",
    )(tokens.T, grad_out.T, w_in.T, short_filter, mr_filter, skip.reshape(1, 64), w_out.T)
    out, taps, gains = pl.pallas_call(
        split_results,
        out_shape=(
            jax.ShapeDtypeStruct((64, ROWS), BF),
            jax.ShapeDtypeStruct((4, TAPS), F32),
            jax.ShapeDtypeStruct((1, 64), F32),
        ),
        in_specs=[vmem],
        out_specs=(vmem, vmem, vmem),
        name="split_results",
    )(sums)
    return out.T, taps, gains.reshape(64)


def solution(mesh):
    in_specs = (
        P("row", "col"),
        P(None, "col"),
        P(None, "col"),
        P("col", None),
        P("col"),
        P(None, "col"),
        P("row", "col"),
    )
    out_specs = (P("row", "col"), P("col", None), P("col"))
    return jax.shard_map(local, mesh=mesh, in_specs=in_specs, out_specs=out_specs, check_vma=False)
```
